1024 devices in a mesh: rows: 64 (over y_hi, z), cols: 16 (over x, y_lo, core).
Axes of the slice: x: 4, y: 4 (y_hi: 2, y_lo: 2; y = y_hi * 2 + y_lo), z: 32, core: 2. Of those that a mesh axis runs over, the one named last changes fastest.
Arguments:
- features: float32 [131072, 256], P(('rows', 'cols')), may hold values from -6 to 6
- degrees: int32 [131072], P(('rows', 'cols')), may hold values from 1 to 16
- tiles: float32 [1024, 24, 128, 128], P(('rows', 'cols')), may hold values from -0.125 to 0.125
- coords: int32 [1024, 24], P(('rows', 'cols')), may hold values from 0 to 16
- counts: int32 [1024], P(('rows', 'cols')), may hold values from 1 to 24, as said below
- weight: float32 [256, 256], replicated, may hold values from -0.375 to 0.375
- cotangent: float32 [131072, 256], P(('rows', 'cols')), may hold values from -6 to 6
Outputs:
- hidden: float32 [131072, 256], P(('rows', 'cols'))
- feature_grad: float32 [131072, 256], P(('rows', 'cols'))
- weight_grad: float32 [256, 256], replicated
The draws below stay inside these ranges and needn't reach their ends.
Inputs may be any that keep to these rules, and one draw needn't show every extreme that they name: `coords`: entries past a slab's count are unused. `counts`: some slab has all 24 tiles live.
All inputs are finite; a program needn't handle non-finite values.
Results may differ from the reference program's by a relative error of at most 0.0003.
Values sent between devices are 32-bit elements; how exact they have to be, the bound alone decides.
A program may use at most 32 MiB of HBM per device.

```python
import jax
import jax.numpy as jnp
from jax import lax

F = 256
TILE = 128
TILES_DEV = 24
DEVICES_ALL = 1024
NODES = 131072
N_ROWS = 64
N_COLS = 16


def draw_counts(key, part):
    key = jax.random.fold_in(key, 11)
    first_key, second_key = jax.random.split(key)
    slabs = NODES // TILE
    values = jax.random.randint(first_key, (slabs,), 1, TILES_DEV + 1)
    chosen = jax.random.randint(second_key, (), 0, slabs)
    return jnp.where(jnp.arange(slabs) == chosen, TILES_DEV, values).astype(jnp.int32)


def with_ends(values, rng, low, high):
    spot = [jax.random.randint(jax.random.fold_in(rng, axis), (), 0, length) for axis, length in enumerate(values.shape)]
    main_axis = values.shape.index(max(values.shape))
    neighbour = spot[:main_axis] + [(spot[main_axis] + 1) % values.shape[main_axis]] + spot[main_axis + 1:]
    return values.at[tuple(spot)].set(low).at[tuple(neighbour)].set(high)


def levels(rng, dims, pieces, least, largest):
    def one(dim, shards_of):
        draws = jax.random.uniform(jax.random.fold_in(jax.random.fold_in(rng, 6), dim), (shards_of,), jnp.float32, least / len(pieces), largest / len(pieces))
        return jnp.repeat(jnp.exp(draws), dims[dim] // shards_of).reshape((-1,) + (1,) * (len(dims) - dim - 1))

    gain = one(*pieces[0])
    for cut in pieces[1:]:
        gain = gain * one(*cut)
    return gain


def scatter_about(own_key, dims, deviation, reach, pieces=(), kind=jnp.bfloat16):
    level = levels(own_key, dims, pieces, -0.22, 0.18) if pieces else 1.0
    values = jax.random.normal(own_key, dims, jnp.float32) * deviation * level
    return jnp.minimum(jnp.maximum(values, -reach), reach).astype(kind)


def setup_inputs(seed: int = 0) -> dict:
    key_of = jax.random.split(jax.random.key(seed), 8)
    return {
        "features": scatter_about(key_of[0], (NODES, F), 1.0, 6.0, ((0, 1024),), jnp.float32),
        "degrees": with_ends(jax.random.randint(key_of[1], (NODES,), 1, 17), jax.random.fold_in(key_of[1], 1), 1, 16).astype(jnp.int32),
        "tiles": scatter_about(key_of[2], (DEVICES_ALL, TILES_DEV, TILE, TILE), (TILE * (N_COLS + 1)) ** -0.5, 0.125, ((0, 1024),), jnp.float32),
        "coords": with_ends(jax.random.randint(key_of[3], (DEVICES_ALL, TILES_DEV), 0, N_COLS + 1), jax.random.fold_in(key_of[3], 1), 0, N_COLS).astype(jnp.int32),
        "counts": draw_counts(jax.random.fold_in(key_of[7], 71), 0),
        "weight": scatter_about(key_of[5], (F, F), F ** -0.5, 0.375, (), jnp.float32),
        "cotangent": scatter_about(key_of[6], (NODES, F), 1.0, 6.0, ((0, 1024),), jnp.float32),
    }


def reference(features, degrees, tiles, coords, counts, weight, cotangent):
    high = lax.Precision.HIGHEST
    norm = 1.0 / jnp.sqrt(degrees.astype(jnp.float32))
    scaled = (features * norm[:, None]).reshape(N_ROWS, N_COLS, TILE, F)
    live = (jnp.arange(TILES_DEV, dtype=jnp.int32)[None, :] < counts[:, None]).astype(jnp.float32)
    tile_grid = tiles.reshape(N_ROWS, N_COLS, TILES_DEV, TILE, TILE)
    coord_grid = coords.reshape(N_ROWS, N_COLS, TILES_DEV)
    live_grid = live.reshape(N_ROWS, N_COLS, TILES_DEV)
    col_ids = jnp.arange(N_COLS, dtype=jnp.int32)

    def forward_row(row_id):
        block = tile_grid[row_id]
        where_col = coord_grid[row_id]
        alive = live_grid[row_id]
        group = scaled[row_id]
        following = scaled[(row_id + 1) % N_ROWS]
        own = group[jnp.minimum(where_col, N_COLS - 1)]
        near = jnp.broadcast_to(following[:, None], own.shape)
        source = jnp.where((where_col == N_COLS)[..., None, None], near, own) * alive[..., None, None]
        return jnp.einsum('ckit,cktf->cif', block, source, precision=high)
    gathered = lax.map(forward_row, jnp.arange(N_ROWS, dtype=jnp.int32))
    aggregated = gathered.reshape(NODES, F) * norm[:, None]
    pre = jnp.dot(aggregated, weight, precision=high)
    gate = jax.nn.sigmoid(pre)
    hidden = pre * gate
    pre_grad = cotangent * gate * (1.0 + pre * (1.0 - gate))
    weight_grad = jnp.dot(aggregated.T, pre_grad, precision=high)
    agg_grad = (jnp.dot(pre_grad, weight.T, precision=high) * norm[:, None]).reshape(N_ROWS, N_COLS, TILE, F)

    def backward_row(row_id):
        block = tile_grid[row_id]
        where_col = coord_grid[row_id]
        alive = live_grid[row_id]
        parts = jnp.einsum('ckit,cif->cktf', block, agg_grad[row_id], precision=high) * alive[..., None, None]
        select = (where_col[..., None] == col_ids[None, None, :]).astype(jnp.float32)
        group_term = jnp.einsum('ckj,cktf->jtf', select, parts, precision=high)
        near_mask = (where_col == N_COLS).astype(jnp.float32)
        near_term = jnp.einsum('ck,cktf->ctf', near_mask, parts, precision=high)
        return (group_term, near_term)
    group_terms, near_terms = lax.map(backward_row, jnp.arange(N_ROWS, dtype=jnp.int32))
    total_grad = group_terms + jnp.roll(near_terms, 1, axis=0)
    feature_grad = total_grad.reshape(NODES, F) * norm[:, None]
    return (hidden, feature_grad, weight_grad)
```

```python
import jax
import jax.numpy as jnp
from jax import lax
from jax.experimental import pallas as pl
from jax.experimental.pallas import tpu as pltpu
from jax.sharding import PartitionSpec as P

F = 256
T = 128
SLOTS = 24
ROWS = 64
NCOLS = 16
HIGH = lax.Precision.HIGHEST
MESH = pl.DeviceIdType.MESH
f32 = jnp.float32

PLANE = [(h, x, y) for h in range(2) for x in range(4) for y in range(2) if (h, x, y) != (0, 0, 0)]
CHIPS = [(x, y) for x in range(4) for y in range(2) if (x, y) != (0, 0)]


def dot(a, b, ca=1, cb=0):
    return lax.dot_general(a, b, (((ca,), (cb,)), ((), ())), precision=HIGH, preferred_element_type=f32)


def kernel(
    deg, coords, counts, feat, tiles, weight, cot,
    hid_o, fg_o, wg_o,
    X, XN, TV, A, FV, WV, CV, NB, AGG, PG, G, HID,
    WP, WR, WS, R1, ZA, ZB, FW,
    TS, TO, RB, RC, TN, RN, FGV,
    lsem, xsend, xrecv, nsend, nrecv, wsend, wrecv, psend, precv,
    zasend, zarecv, zbsend, zbrecv, fsend, frecv, tsend, trecv, csend, crecv, osem, chain,
):
    r = lax.axis_index("rows")
    c = lax.axis_index("cols")
    h, z = r // 32, r % 32
    x, y, k = c // 4, (c // 2) % 2, c % 2

    def dev(dh=0, dx=0, dy=0, dc=0, dz=0):
        row = ((h + dh) % 2) * 32 + (z + dz) % 32
        col = ((x + dx) % 4) * 4 + ((y + dy) % 2) * 2 + (k + dc) % 2
        return row, col

    def slot(dx=0, dy=0, dc=0):
        return ((x + dx) % 4) * 4 + ((y + dy) % 2) * 2 + (k + dc) % 2

    def remote(src, dst, ss, rs, to):
        return pltpu.make_async_remote_copy(
            src_ref=src, dst_ref=dst, send_sem=ss, recv_sem=rs, device_id=to, device_id_type=MESH
        )

    pending = []

    def start(src, dst, ss, rs, to):
        cp = remote(src, dst, ss, rs, to)
        cp.start()
        pending.append(cp)

    SIB = dev(dc=1)
    nxt = ((r + 1) % ROWS, c)
    prv = ((r + ROWS - 1) % ROWS, c)

    loads = [
        pltpu.make_async_copy(feat, FV, lsem.at[0]),
        pltpu.make_async_copy(tiles, TV, lsem.at[1]),
        pltpu.make_async_copy(weight, WV, lsem.at[2]),
        pltpu.make_async_copy(cot, CV, lsem.at[3]),
    ]
    for cp in loads:
        cp.start()

    barrier = pltpu.get_barrier_semaphore()
    greet = [dev(dh=a, dx=b, dy=d) for a, b, d in PLANE]
    greet += [SIB, nxt, prv, dev(dz=1), dev(dz=31)]
    for to in greet:
        pl.semaphore_signal(barrier, inc=1, device_id=to, device_id_type=MESH)

    nrow = 1.0 / jnp.sqrt(deg[...].astype(f32))
    eye = lax.broadcasted_iota(jnp.int32, (T, T), 0) == lax.broadcasted_iota(jnp.int32, (T, T), 1)
    norm = jnp.sum(jnp.where(eye, jnp.broadcast_to(nrow, (T, T)), 0.0), axis=1, keepdims=True)
    NB[...] = jnp.broadcast_to(norm, (T, F))
    me = slot()
    loads[0].wait()
    X[me] = FV[...] * NB[...]
    pl.semaphore_wait(barrier, len(greet))

    half = T // 2

    def piece(sl, hf):
        return X.at[sl, pl.ds(hf * half, half)]

    def send(sl, hf, to):
        start(piece(sl, hf), piece(sl, hf), xsend.at[len(pending)], xrecv.at[sl, hf], to)

    def recv(sl, hf):
        remote(piece(sl, hf), piece(sl, hf), xsend.at[0], xrecv.at[sl, hf], SIB).wait_recv()

    def step(level):
        if level > 0:
            pl.semaphore_wait(chain.at[level - 1], 2)
        if level < 4:
            d = 2 ** level
            for dz in (d, 32 - d):
                pl.semaphore_signal(chain.at[level], inc=1, device_id=dev(dz=dz), device_id_type=MESH)

    def use(sl):
        AGG[...] += dot(A[sl], X[sl])

    R, L, Y = dev(dx=1), dev(dx=3), dev(dy=1)
    send(me, 0, Y)
    send(me, 1, Y)
    send(me, 0, R)
    send(me, 1, L)
    send(me, 1, R)
    send(me, 0, L)
    for hf in (0, 1):
        send(me, hf, SIB)
    start(X.at[me], XN, nsend.at[0], nrecv.at[0], prv)
    step(0)

    loads[1].wait()
    live = counts[0]

    def build(j, carry):
        acc = jnp.zeros((T, T), f32)
        for t in range(SLOTS):
            on = jnp.logical_and(coords[0, t] == j, t < live)
            acc = acc + jnp.where(on, 1.0, 0.0) * TV[t]
        A[j] = acc
        return carry

    lax.fori_loop(0, NCOLS + 1, build, 0)
    AGG[...] = dot(A[me], X[me])

    ys = slot(dy=1)
    recv(ys, 0)
    send(ys, 0, R)
    recv(ys, 1)
    send(ys, 1, L)
    send(ys, 1, R)
    send(ys, 0, L)
    for hf in (0, 1):
        send(ys, hf, SIB)
    step(1)
    done = [ys]
    for dy in (0, 1):
        a, b = slot(dx=3, dy=dy), slot(dx=1, dy=dy)
        recv(a, 0)
        send(a, 0, R)
        recv(b, 1)
        send(b, 1, L)
        send(a, 0, SIB)
        send(b, 1, SIB)
        recv(a, 1)
        send(a, 1, SIB)
        recv(b, 0)
        send(b, 0, SIB)
        step(2 + dy)
        for sl in done:
            use(sl)
        done = [a, b]
    for dy in (0, 1):
        sl = slot(dx=2, dy=dy)
        for hf in (0, 1):
            recv(sl, hf)
            send(sl, hf, SIB)
        done.append(sl)
    for sl in done:
        use(sl)
    remote(X.at[me], XN, nsend.at[0], nrecv.at[0], prv).wait_recv()
    AGG[...] += dot(A[NCOLS], XN[...])
    for dx, dy in [(0, 0), (0, 1), (3, 0), (1, 0), (3, 1), (1, 1), (2, 0), (2, 1)]:
        sl = slot(dx=dx, dy=dy, dc=1)
        for hf in (0, 1):
            recv(sl, hf)
        use(sl)

    loads[2].wait()
    loads[3].wait()
    agg = AGG[...] * NB[...]
    pre = dot(agg, WV[...])
    gate = jax.nn.sigmoid(pre)
    HID[...] = pre * gate
    hid_copy = pltpu.make_async_copy(HID, hid_o, osem.at[0])
    hid_copy.start()
    pg = CV[...] * gate * (1.0 + pre * (1.0 - gate))
    PG[...] = pg
    wg = dot(agg, pg, 0, 0)
    WP[0] = wg[:T]
    WP[1] = wg[T:]
    start(WP.at[1 - k], WR, wsend.at[0], wrecv.at[0], SIB)
    G[...] = dot(PG[...], WV[...], 1, 1) * NB[...]
    TN[...] = dot(A[NCOLS], G[...], 0, 0)
    start(TN, RN, nsend.at[1], nrecv.at[1], nxt)
    remote(WP.at[0], WR, wsend.at[0], wrecv.at[0], SIB).wait_recv()
    WS[...] = (WP[k] + WR[...]).reshape(16, 8, F)

    def plane_id(dh=0, dx=0, dy=0):
        return ((x + dx) % 4) * 4 + ((h + dh) % 2) * 2 + (y + dy) % 2

    q = plane_id()
    for i, (a, b, d) in enumerate(PLANE):
        start(WS.at[plane_id(a, b, d)], R1.at[i], psend.at[i], precv.at[i], dev(dh=a, dx=b, dy=d))

    for p in range(8):
        TS[p] = dot(A[p * 2 + 1 - k], G[...], 0, 0)
        start(TS.at[p], RB.at[p], tsend.at[p], trecv.at[p], SIB)
    for p in range(8):
        TO[p] = dot(A[p * 2 + k], G[...], 0, 0)

    for i in range(15):
        remote(WS.at[0], R1.at[i], psend.at[i], precv.at[i], SIB).wait_recv()
    total = WS[q]
    for i in range(15):
        total = total + R1[i]
    z4, zs = z % 4, z // 4
    ZA[z4] = total
    for i in range(1, 4):
        m = (z4 + i) % 4
        start(ZA.at[z4], ZA.at[z4], zasend.at[i - 1], zarecv.at[z4], (h * 32 + zs * 4 + m, c))
    step(4)
    for p in range(8):
        remote(TS.at[p], RB.at[p], tsend.at[p], trecv.at[p], SIB).wait_recv()
        TO[p] = TO[p] + RB[p]
    for i in range(1, 4):
        m = (z4 + i) % 4
        remote(ZA.at[m], ZA.at[m], zasend.at[0], zarecv.at[m], SIB).wait_recv()
    ZB[zs] = ((ZA[0] + ZA[1]) + (ZA[2] + ZA[3]))
    for i in range(1, 8):
        start(ZB.at[zs], ZB.at[zs], zbsend.at[i - 1], zbrecv.at[zs], dev(dz=4 * i))

    cp_id = x * 2 + y
    for i, (dx, dy) in enumerate(CHIPS):
        to = ((x + dx) % 4) * 2 + (y + dy) % 2
        start(TO.at[to], RC.at[i], csend.at[i], crecv.at[i], dev(dx=dx, dy=dy))

    for i in range(1, 8):
        m = (zs + i) % 8
        remote(ZB.at[m], ZB.at[m], zbsend.at[0], zbrecv.at[m], SIB).wait_recv()
    total = ZB[0]
    for i in range(1, 8):
        total = total + ZB[i]
    FW[k * 16 + q] = total
    mine = FW.at[k * 16 + q]
    for i, (a, b, d) in enumerate(PLANE):
        start(mine, mine, fsend.at[i], frecv.at[q], dev(dh=a, dx=b, dy=d))

    remote(TN, RN, nsend.at[1], nrecv.at[1], nxt).wait_recv()
    for i in range(7):
        remote(TO.at[0], RC.at[i], csend.at[i], crecv.at[i], SIB).wait_recv()
    fg = TO[cp_id] + RN[...]
    for i in range(7):
        fg = fg + RC[i]
    FGV[...] = fg * NB[...]
    fg_copy = pltpu.make_async_copy(FGV, fg_o, osem.at[1])
    fg_copy.start()

    for a, b, d in PLANE:
        o = plane_id(a, b, d)
        part = FW.at[k * 16 + o]
        remote(part, part, fsend.at[0], frecv.at[o], SIB).wait_recv()
    block = FW.at[pl.ds(k * 16, 16)]
    start(block, block, wsend.at[1], wrecv.at[1], SIB)
    other = FW.at[pl.ds((1 - k) * 16, 16)]
    remote(other, other, wsend.at[1], wrecv.at[1], SIB).wait_recv()
    wg_copy = pltpu.make_async_copy(FW, wg_o, osem.at[2])
    wg_copy.start()
    hid_copy.wait()
    fg_copy.wait()
    for cp in pending:
        cp.wait_send()
    wg_copy.wait()


def local(features, degrees, tiles, coords, counts, weight, cotangent):
    anyspace = pl.BlockSpec(memory_space=pl.ANY)
    smem = pl.BlockSpec(memory_space=pltpu.SMEM)
    vmem = pl.BlockSpec(memory_space=pltpu.VMEM)
    D = pltpu.SemaphoreType.DMA
    V = lambda *s: pltpu.VMEM(s, f32)
    hidden, feature_grad, weight_grad = pl.pallas_call(
        kernel,
        out_shape=(
            jax.ShapeDtypeStruct((T, F), f32),
            jax.ShapeDtypeStruct((T, F), f32),
            jax.ShapeDtypeStruct((32, 8, F), f32),
        ),
        in_specs=[vmem, smem, smem, anyspace, anyspace, anyspace, anyspace],
        out_specs=(anyspace, anyspace, anyspace),
        scratch_shapes=[
            V(NCOLS, T, F), V(T, F), V(SLOTS, T, T), V(NCOLS + 1, T, T), V(T, F), V(F, F), V(T, F),
            V(T, F), V(T, F), V(T, F), V(T, F), V(T, F),
            V(2, T, F), V(T, F), V(16, 8, F), V(15, 8, F), V(4, 8, F), V(8, 8, F), V(32, 8, F),
            V(8, T, F), V(8, T, F), V(8, T, F), V(7, T, F), V(T, F), V(T, F), V(T, F),
            D((4,)), D((48,)), D((NCOLS, 2)), D((2,)), D((2,)), D((2,)), D((2,)), D((15,)), D((15,)),
            D((3,)), D((4,)), D((7,)), D((8,)), D((15,)), D((16,)), D((8,)), D((8,)), D((7,)), D((7,)),
            D((3,)), pltpu.SemaphoreType.REGULAR((4,)),
        ],
        compiler_params=pltpu.CompilerParams(
            collective_id=1, has_side_effects=True, vmem_limit_bytes=60 << 20
        ),
        cost_estimate=pl.CostEstimate(flops=400_000_000, bytes_accessed=3_000_000, transcendentals=32768),
        name="layer",
    )(degrees.reshape(1, T), coords, counts, features, tiles.reshape(SLOTS, T, T), weight, cotangent)
    return hidden, feature_grad, weight_grad.reshape(F, F)


def solution(mesh):
    return jax.shard_map(
        local,
        mesh=mesh,
        in_specs=(
            P(("rows", "cols"), None),
            P(("rows", "cols")),
            P(("rows", "cols"), None, None, None),
            P(("rows", "cols"), None),
            P(("rows", "cols")),
            P(),
            P(("rows", "cols"), None),
        ),
        out_specs=(P(("rows", "cols"), None), P(("rows", "cols"), None), P()),
        check_vma=False,
    )
```

```python
import jax
import jax.numpy as jnp
from jax import lax
from jax.experimental import pallas as pl
from jax.experimental.pallas import tpu as pltpu
from jax.sharding import PartitionSpec as P

F = 256
T = 128
SLOTS = 24
ROWS = 64
NCOLS = 16
HIGH = lax.Precision.HIGHEST
MESH = pl.DeviceIdType.MESH
f32 = jnp.float32

PLANE = [(h, x, y) for h in range(2) for x in range(4) for y in range(2) if (h, x, y) != (0, 0, 0)]
PLANE.sort(key=lambda p: -(2 * p[0] + min(p[1], 4 - p[1]) + (p[2] if not p[0] else 0)))
FAR = [4, 3, 5, 2, 6, 1, 7]
CHIPS = [(x, y) for x in range(4) for y in range(2) if (x, y) != (0, 0)]


def dot(a, b, ca=1, cb=0):
    return lax.dot_general(a, b, (((ca,), (cb,)), ((), ())), precision=HIGH, preferred_element_type=f32)


def kernel(
    deg_i, coords_i, counts_i, feat, tiles, weight, cot,
    hid_o, fg_o, wg_o,
    deg, coords, counts, X, XN, TV, A, FV, WV, CV, NB, AGG, PG, G, HID,
    WP, WR, WS, R1, ZA, ZB, FW,
    TS, TO, RB, RC, TN, RN, FGV,
    lsem, xsend, xrecv, nsend, nrecv, wsend, wrecv, psend, precv,
    zasend, zarecv, zbsend, zbrecv, fsend, frecv, tsend, trecv, csend, crecv, osem, chain, pchain,
):
    r = lax.axis_index("rows")
    c = lax.axis_index("cols")
    h, z = r // 32, r % 32
    x, y, k = c // 4, (c // 2) % 2, c % 2

    def dev(dh=0, dx=0, dy=0, dc=0, dz=0):
        row = ((h + dh) % 2) * 32 + (z + dz) % 32
        col = ((x + dx) % 4) * 4 + ((y + dy) % 2) * 2 + (k + dc) % 2
        return row, col

    def slot(dx=0, dy=0, dc=0):
        return ((x + dx) % 4) * 4 + ((y + dy) % 2) * 2 + (k + dc) % 2

    def remote(src, dst, ss, rs, to):
        return pltpu.make_async_remote_copy(
            src_ref=src, dst_ref=dst, send_sem=ss, recv_sem=rs, device_id=to, device_id_type=MESH
        )

    pending = []

    def start(src, dst, ss, rs, to):
        cp = remote(src, dst, ss, rs, to)
        cp.start()
        pending.append(cp)

    SIB = dev(dc=1)
    nxt = ((r + 1) % ROWS, c)
    prv = ((r + ROWS - 1) % ROWS, c)

    loads = [
        pltpu.make_async_copy(feat, FV, lsem.at[0]),
        pltpu.make_async_copy(tiles, TV, lsem.at[1]),
        pltpu.make_async_copy(weight, WV, lsem.at[2]),
        pltpu.make_async_copy(cot, CV, lsem.at[3]),
        pltpu.make_async_copy(deg_i, deg, lsem.at[4]),
        pltpu.make_async_copy(coords_i, coords, lsem.at[5]),
        pltpu.make_async_copy(counts_i, counts, lsem.at[6]),
    ]
    for i in (4, 0):
        loads[i].start()

    barrier = pltpu.get_barrier_semaphore()
    R, L, Y, H = dev(dx=1), dev(dx=3), dev(dy=1), dev(dh=1)
    greet = [H, R, L, Y, nxt, prv, dev(dz=1), dev(dz=31), SIB]
    for to in greet:
        pl.semaphore_signal(barrier, inc=1, device_id=to, device_id_type=MESH)

    for i in (1, 5, 6, 2, 3):
        loads[i].start()
    loads[4].wait()
    nrow = 1.0 / jnp.sqrt(deg[...].astype(f32))
    eye = lax.broadcasted_iota(jnp.int32, (T, T), 0) == lax.broadcasted_iota(jnp.int32, (T, T), 1)
    norm = jnp.sum(jnp.where(eye, jnp.broadcast_to(nrow, (T, T)), 0.0), axis=1, keepdims=True)
    NB[...] = jnp.broadcast_to(norm, (T, F))
    me = slot()
    loads[0].wait()
    X[me] = FV[...] * NB[...]
    pl.semaphore_wait(barrier, len(greet))

    half = T // 2

    def piece(sl, hf):
        return X.at[sl, pl.ds(hf * half, half)]

    def send(sl, hf, to):
        start(piece(sl, hf), piece(sl, hf), xsend.at[len(pending)], xrecv.at[sl, hf], to)

    def recv(sl, hf):
        remote(piece(sl, hf), piece(sl, hf), xsend.at[0], xrecv.at[sl, hf], SIB).wait_recv()

    def step(level):
        if level > 0:
            pl.semaphore_wait(chain.at[level - 1], 2)
        if level < 4:
            d = 2 ** level
            for dz in (d, 32 - d):
                pl.semaphore_signal(chain.at[level], inc=1, device_id=dev(dz=dz), device_id_type=MESH)

    def plane_step(level):
        if level > 0:
            pl.semaphore_wait(pchain.at[level - 1], (4, 2)[level - 1])
        if level < 2:
            for to in ((R, L, Y, H), (dev(dh=1, dy=1), dev(dx=2)))[level]:
                pl.semaphore_signal(pchain.at[level], inc=1, device_id=to, device_id_type=MESH)

    def send_all(sl, to):
        start(X.at[sl], X.at[sl], xsend.at[len(pending)], xrecv.at[sl, 0], to)

    def recv_all(sl):
        remote(X.at[sl], X.at[sl], xsend.at[0], xrecv.at[sl, 0], SIB).wait_recv()

    def use(sl):
        AGG[...] += dot(A[sl], X[sl])

    send(me, 0, Y)
    send(me, 1, Y)
    send(me, 0, R)
    send(me, 1, L)
    send(me, 1, R)
    send(me, 0, L)
    send_all(me, SIB)
    start(X.at[me], XN, nsend.at[0], nrecv.at[0], prv)
    step(0)
    plane_step(0)

    for i in (1, 5, 6):
        loads[i].wait()
    live = counts[0]

    def build(j, carry):
        acc = jnp.zeros((T, T), f32)
        for t in range(SLOTS):
            on = jnp.logical_and(coords[0, t] == j, t < live)
            acc = acc + jnp.where(on, 1.0, 0.0) * TV[t]
        A[j] = acc
        return carry

    lax.fori_loop(0, NCOLS + 1, build, 0)
    AGG[...] = dot(A[me], X[me])

    ys = slot(dy=1)
    recv(ys, 0)
    send(ys, 0, R)
    recv(ys, 1)
    send(ys, 1, L)
    send(ys, 1, R)
    send(ys, 0, L)
    send_all(ys, SIB)
    done = [ys]
    for dy in (0, 1):
        a, b = slot(dx=3, dy=dy), slot(dx=1, dy=dy)
        recv(a, 0)
        send(a, 0, R)
        recv(b, 1)
        send(b, 1, L)
        recv(a, 1)
        send_all(a, SIB)
        recv(b, 0)
        send_all(b, SIB)
        step(1 + dy)
        if dy == 0:
            plane_step(1)
        for sl in done:
            use(sl)
        done = [a, b]
    for dy in (0, 1):
        sl = slot(dx=2, dy=dy)
        for hf in (0, 1):
            recv(sl, hf)
            send(sl, hf, SIB)
        done.append(sl)
    step(3)
    for sl in done:
        use(sl)
    remote(X.at[me], XN, nsend.at[0], nrecv.at[0], prv).wait_recv()
    AGG[...] += dot(A[NCOLS], XN[...])
    for dx, dy in [(0, 0), (0, 1), (3, 0), (1, 0), (3, 1), (1, 1), (2, 0), (2, 1)]:
        sl = slot(dx=dx, dy=dy, dc=1)
        if dx == 2:
            for hf in (0, 1):
                recv(sl, hf)
        else:
            recv_all(sl)
        use(sl)

    loads[2].wait()
    loads[3].wait()
    agg = AGG[...] * NB[...]
    pre = dot(agg, WV[...])
    gate = jax.nn.sigmoid(pre)
    HID[...] = pre * gate
    hid_copy = pltpu.make_async_copy(HID, hid_o, osem.at[0])
    hid_copy.start()
    pg = CV[...] * gate * (1.0 + pre * (1.0 - gate))
    PG[...] = pg
    wg = dot(agg, pg, 0, 0)
    WP[0] = wg[:T]
    WP[1] = wg[T:]
    start(WP.at[1 - k], WR, wsend.at[0], wrecv.at[0], SIB)
    G[...] = dot(PG[...], WV[...], 1, 1) * NB[...]
    TN[...] = dot(A[NCOLS], G[...], 0, 0)
    start(TN, RN, nsend.at[1], nrecv.at[1], nxt)
    remote(WP.at[0], WR, wsend.at[0], wrecv.at[0], SIB).wait_recv()
    WS[...] = (WP[k] + WR[...]).reshape(16, 8, F)

    def plane_id(dh=0, dx=0, dy=0):
        return ((x + dx) % 4) * 4 + ((h + dh) % 2) * 2 + (y + dy) % 2

    plane_step(2)
    q = plane_id()
    for i, (a, b, d) in enumerate(PLANE):
        start(WS.at[plane_id(a, b, d)], R1.at[i], psend.at[i], precv.at[i], dev(dh=a, dx=b, dy=d))

    for p in range(8):
        TS[p] = dot(A[p * 2 + 1 - k], G[...], 0, 0)
        start(TS.at[p], RB.at[p], tsend.at[p], trecv.at[p], SIB)
    for p in range(8):
        TO[p] = dot(A[p * 2 + k], G[...], 0, 0)

    for i in range(15):
        remote(WS.at[0], R1.at[i], psend.at[i], precv.at[i], SIB).wait_recv()
    total = WS[q]
    for i in range(15):
        total = total + R1[i]
    z4, zs = z % 4, z // 4
    ZA[z4] = total
    for i in (2, 3, 1):
        m = (z4 + i) % 4
        start(ZA.at[z4], ZA.at[z4], zasend.at[i - 1], zarecv.at[z4], (h * 32 + zs * 4 + m, c))
    step(4)
    for p in range(8):
        remote(TS.at[p], RB.at[p], tsend.at[p], trecv.at[p], SIB).wait_recv()
        TO[p] = TO[p] + RB[p]
    for i in range(1, 4):
        m = (z4 + i) % 4
        remote(ZA.at[m], ZA.at[m], zasend.at[0], zarecv.at[m], SIB).wait_recv()
    ZB[zs] = ((ZA[0] + ZA[1]) + (ZA[2] + ZA[3]))
    for i in FAR:
        start(ZB.at[zs], ZB.at[zs], zbsend.at[i - 1], zbrecv.at[zs], dev(dz=4 * i))

    cp_id = x * 2 + y
    for i, (dx, dy) in enumerate(CHIPS):
        to = ((x + dx) % 4) * 2 + (y + dy) % 2
        start(TO.at[to], RC.at[i], csend.at[i], crecv.at[i], dev(dx=dx, dy=dy))

    for i in range(1, 8):
        m = (zs + i) % 8
        remote(ZB.at[m], ZB.at[m], zbsend.at[0], zbrecv.at[m], SIB).wait_recv()
    total = ZB[0]
    for i in range(1, 8):
        total = total + ZB[i]
    FW[...] = total
    own = pltpu.make_async_copy(FW, wg_o.at[k * 16 + q], osem.at[2])
    own.start()
    mine = wg_o.at[k * 16 + q]
    for i, (a, b, d) in enumerate(PLANE):
        start(FW, mine, fsend.at[i], frecv.at[q], dev(dh=a, dx=b, dy=d))

    remote(TN, RN, nsend.at[1], nrecv.at[1], nxt).wait_recv()
    for i in range(7):
        remote(TO.at[0], RC.at[i], csend.at[i], crecv.at[i], SIB).wait_recv()
    fg = TO[cp_id] + RN[...]
    for i in range(7):
        fg = fg + RC[i]
    FGV[...] = fg * NB[...]
    fg_copy = pltpu.make_async_copy(FGV, fg_o, osem.at[1])
    fg_copy.start()

    for a, b, d in PLANE:
        o = plane_id(a, b, d)
        part = wg_o.at[k * 16 + o]
        remote(part, part, fsend.at[0], frecv.at[o], SIB).wait_recv()
    own.wait()
    block = wg_o.at[pl.ds(k * 16, 16)]
    start(block, block, wsend.at[1], wrecv.at[1], SIB)
    other = wg_o.at[pl.ds((1 - k) * 16, 16)]
    remote(other, other, wsend.at[1], wrecv.at[1], SIB).wait_recv()
    hid_copy.wait()
    fg_copy.wait()
    for cp in pending:
        cp.wait_send()


def local(features, degrees, tiles, coords, counts, weight, cotangent):
    anyspace = pl.BlockSpec(memory_space=pl.ANY)
    D = pltpu.SemaphoreType.DMA
    V = lambda *s: pltpu.VMEM(s, f32)
    hidden, feature_grad, weight_grad = pl.pallas_call(
        kernel,
        out_shape=(pltpu.VMEM((T, F), f32), pltpu.VMEM((T, F), f32), pltpu.VMEM((32, 8, F), f32)),
        in_specs=[pl.BlockSpec(memory_space=pltpu.HBM)] * 7,
        out_specs=(anyspace, anyspace, anyspace),
        scratch_shapes=[
            pltpu.VMEM((1, T), jnp.int32), pltpu.SMEM((1, SLOTS), jnp.int32), pltpu.SMEM((1,), jnp.int32),
            V(NCOLS, T, F), V(T, F), V(SLOTS, T, T), V(NCOLS + 1, T, T), V(T, F), V(F, F), V(T, F),
            V(T, F), V(T, F), V(T, F), V(T, F), V(T, F),
            V(2, T, F), V(T, F), V(16, 8, F), V(15, 8, F), V(4, 8, F), V(8, 8, F), V(8, F),
            V(8, T, F), V(8, T, F), V(8, T, F), V(7, T, F), V(T, F), V(T, F), V(T, F),
            D((7,)), D((48,)), D((NCOLS, 2)), D((2,)), D((2,)), D((2,)), D((2,)), D((15,)), D((15,)),
            D((3,)), D((4,)), D((7,)), D((8,)), D((15,)), D((16,)), D((8,)), D((8,)), D((7,)), D((7,)),
            D((3,)), pltpu.SemaphoreType.REGULAR((4,)), pltpu.SemaphoreType.REGULAR((2,)),
        ],
        compiler_params=pltpu.CompilerParams(
            collective_id=1, has_side_effects=True, vmem_limit_bytes=60 << 20
        ),
        cost_estimate=pl.CostEstimate(flops=400_000_000, bytes_accessed=3_000_000, transcendentals=32768),
        name="layer",
    )(degrees.reshape(1, T), coords, counts, features, tiles.reshape(SLOTS, T, T), weight, cotangent)
    return hidden, feature_grad, weight_grad.reshape(F, F)


def solution(mesh):
    return jax.shard_map(
        local,
        mesh=mesh,
        in_specs=(
            P(("rows", "cols"), None),
            P(("rows", "cols")),
            P(("rows", "cols"), None, None, None),
            P(("rows", "cols"), None),
            P(("rows", "cols")),
            P(),
            P(("rows", "cols"), None),
        ),
        out_specs=(P(("rows", "cols"), None), P(("rows", "cols"), None), P()),
        check_vma=False,
    )
```

```python
import jax
import jax.numpy as jnp
from jax import lax
from jax.experimental import pallas as pl
from jax.experimental.pallas import tpu as pltpu
from jax.sharding import PartitionSpec as P

F = 256
T = 128
SLOTS = 24
ROWS = 64
NCOLS = 16
MESH = pl.DeviceIdType.MESH
f32 = jnp.float32

PLANE = [(h, x, y) for h in range(2) for x in range(4) for y in range(2) if (h, x, y) != (0, 0, 0)]
PLANE.sort(key=lambda p: -(2 * p[0] + min(p[1], 4 - p[1]) + (p[2] if not p[0] else 0)))
FAR = [4, 3, 5, 2, 6, 1, 7]
CHIPS = [(x, y) for x in range(4) for y in range(2) if (x, y) != (0, 0)]


def split(v):
    top = v.astype(jnp.bfloat16)
    return top, (v - top.astype(f32)).astype(jnp.bfloat16)


def dot(a, b, ca=1, cb=0):
    def one(u, v):
        return lax.dot_general(u, v, (((ca,), (cb,)), ((), ())), preferred_element_type=f32)

    return one(a[0], b[0]) + (one(a[0], b[1]) + one(a[1], b[0]))


def kernel(
    deg_i, coords_i, counts_i, feat, tiles, weight, cot,
    hid_o, fg_o, wg_o,
    deg, coords, counts, X, XN, TV, A1, A2, FV, WV, CV, NB, AGG, W1, W2, G1, G2, HID,
    WP, WR, WS, R1, ZA, ZB, FW,
    TS, TO, RB, RC, TN, RN, FGV,
    lsem, xsend, xrecv, nsend, nrecv, wsend, wrecv, psend, precv,
    zasend, zarecv, zbsend, zbrecv, fsend, frecv, tsend, trecv, csend, crecv, osem, chain, pchain,
):
    r = lax.axis_index("rows")
    c = lax.axis_index("cols")
    h, z = r // 32, r % 32
    x, y, k = c // 4, (c // 2) % 2, c % 2

    def dev(dh=0, dx=0, dy=0, dc=0, dz=0):
        row = ((h + dh) % 2) * 32 + (z + dz) % 32
        col = ((x + dx) % 4) * 4 + ((y + dy) % 2) * 2 + (k + dc) % 2
        return row, col

    def slot(dx=0, dy=0, dc=0):
        return ((x + dx) % 4) * 4 + ((y + dy) % 2) * 2 + (k + dc) % 2

    def remote(src, dst, ss, rs, to):
        return pltpu.make_async_remote_copy(
            src_ref=src, dst_ref=dst, send_sem=ss, recv_sem=rs, device_id=to, device_id_type=MESH
        )

    pending = []

    def start(src, dst, ss, rs, to):
        cp = remote(src, dst, ss, rs, to)
        cp.start()
        pending.append(cp)

    def settle(count):
        for cp in pending[-count:]:
            cp.wait_send()
        del pending[-count:]

    SIB = dev(dc=1)
    nxt = ((r + 1) % ROWS, c)
    prv = ((r + ROWS - 1) % ROWS, c)

    loads = [
        pltpu.make_async_copy(feat, FV, lsem.at[0]),
        pltpu.make_async_copy(tiles, TV, lsem.at[1]),
        pltpu.make_async_copy(weight, WV, lsem.at[2]),
        pltpu.make_async_copy(cot, CV, lsem.at[3]),
        pltpu.make_async_copy(deg_i, deg, lsem.at[4]),
        pltpu.make_async_copy(coords_i, coords, lsem.at[5]),
        pltpu.make_async_copy(counts_i, counts, lsem.at[6]),
    ]
    for i in (4, 0):
        loads[i].start()

    barrier = pltpu.get_barrier_semaphore()
    R, L, Y, H = dev(dx=1), dev(dx=3), dev(dy=1), dev(dh=1)
    greet = [H, R, L, Y, nxt, prv, dev(dz=1), dev(dz=31), SIB]
    for to in greet:
        pl.semaphore_signal(barrier, inc=1, device_id=to, device_id_type=MESH)

    for i in (1, 5, 6, 2, 3):
        loads[i].start()
    loads[4].wait()
    nrow = 1.0 / jnp.sqrt(deg[...].astype(f32))
    eye = lax.broadcasted_iota(jnp.int32, (T, T), 0) == lax.broadcasted_iota(jnp.int32, (T, T), 1)
    norm = jnp.sum(jnp.where(eye, jnp.broadcast_to(nrow, (T, T)), 0.0), axis=1, keepdims=True)
    NB[...] = jnp.broadcast_to(norm, (T, F))
    me = slot()
    loads[0].wait()
    X[me] = FV[...] * NB[...]
    pl.semaphore_wait(barrier, len(greet))

    half = T // 2

    def piece(sl, hf):
        return X.at[sl, pl.ds(hf * half, half)]

    def send(sl, hf, to):
        start(piece(sl, hf), piece(sl, hf), xsend.at[len(pending)], xrecv.at[sl, hf], to)

    def recv(sl, hf):
        remote(piece(sl, hf), piece(sl, hf), xsend.at[0], xrecv.at[sl, hf], SIB).wait_recv()

    def step(level):
        if level > 0:
            pl.semaphore_wait(chain.at[level - 1], 2)
        if level < 4:
            d = 2 ** level
            for dz in (d, 32 - d):
                pl.semaphore_signal(chain.at[level], inc=1, device_id=dev(dz=dz), device_id_type=MESH)

    def plane_step(level):
        if level > 0:
            pl.semaphore_wait(pchain.at[level - 1], (4, 2)[level - 1])
        if level < 2:
            for to in ((R, L, Y, H), (dev(dh=1, dy=1), dev(dx=2)))[level]:
                pl.semaphore_signal(pchain.at[level], inc=1, device_id=to, device_id_type=MESH)

    def send_all(sl, to):
        start(X.at[sl], X.at[sl], xsend.at[len(pending)], xrecv.at[sl, 0], to)

    def recv_all(sl):
        remote(X.at[sl], X.at[sl], xsend.at[0], xrecv.at[sl, 0], SIB).wait_recv()

    def block(j):
        return A1[j], A2[j]

    def use(sl):
        AGG[...] += dot(block(sl), split(X[sl]))

    send(me, 0, Y)
    send(me, 1, Y)
    send(me, 0, R)
    send(me, 1, L)
    send(me, 1, R)
    send(me, 0, L)
    send_all(me, SIB)
    start(X.at[me], XN, nsend.at[0], nrecv.at[0], prv)
    step(0)
    plane_step(0)

    for i in (1, 5, 6):
        loads[i].wait()
    live = counts[0]

    def build(j, carry):
        acc = jnp.zeros((T, T), f32)
        for t in range(SLOTS):
            on = jnp.logical_and(coords[0, t] == j, t < live)
            acc = acc + jnp.where(on, 1.0, 0.0) * TV[t]
        A1[j], A2[j] = split(acc)
        return carry

    lax.fori_loop(0, NCOLS + 1, build, 0)
    AGG[...] = dot(block(me), split(X[me]))
    loads[2].wait()
    W1[...], W2[...] = split(WV[...])
    loads[3].wait()

    ys = slot(dy=1)
    recv(ys, 0)
    send(ys, 0, R)
    recv(ys, 1)
    send(ys, 1, L)
    send(ys, 1, R)
    send(ys, 0, L)
    send_all(ys, SIB)
    done = [ys]
    for dy in (0, 1):
        a, b = slot(dx=3, dy=dy), slot(dx=1, dy=dy)
        recv(a, 0)
        send(a, 0, R)
        recv(b, 1)
        send(b, 1, L)
        recv(a, 1)
        send_all(a, SIB)
        recv(b, 0)
        send_all(b, SIB)
        step(1 + dy)
        if dy == 0:
            plane_step(1)
        for sl in done:
            use(sl)
        done = [a, b]
    for dy in (0, 1):
        sl = slot(dx=2, dy=dy)
        for hf in (0, 1):
            recv(sl, hf)
            send(sl, hf, SIB)
        done.append(sl)
    step(3)
    for sl in done:
        use(sl)
    remote(X.at[me], XN, nsend.at[0], nrecv.at[0], prv).wait_recv()
    AGG[...] += dot(block(NCOLS), split(XN[...]))
    for dx, dy in [(0, 0), (0, 1), (3, 0), (1, 0), (3, 1), (1, 1), (2, 0), (2, 1)]:
        sl = slot(dx=dx, dy=dy, dc=1)
        if dx == 2:
            for hf in (0, 1):
                recv(sl, hf)
        else:
            recv_all(sl)
        use(sl)

    agg = AGG[...] * NB[...]
    wparts = W1[...], W2[...]
    pre = dot(split(agg), wparts)
    gate = jax.nn.sigmoid(pre)
    pg = split(CV[...] * gate * (1.0 + pre * (1.0 - gate)))
    first, second = split(agg[:, :T]), split(agg[:, T:])
    theirs = [jnp.where(k == 0, u, v) for u, v in zip(second, first)]
    own = [jnp.where(k == 0, u, v) for u, v in zip(first, second)]
    WP[...] = dot(theirs, pg, 0, 0)
    start(WP, WR, wsend.at[0], wrecv.at[0], SIB)
    mine = dot(own, pg, 0, 0)
    HID[...] = pre * gate
    hid_copy = pltpu.make_async_copy(HID, hid_o, osem.at[0])
    hid_copy.start()
    g = split(dot(pg, wparts, 1, 1) * NB[...])
    G1[...], G2[...] = g
    remote(WP, WR, wsend.at[0], wrecv.at[0], SIB).wait_recv()
    WS[...] = (mine + WR[...]).reshape(16, 8, F)

    def plane_id(dh=0, dx=0, dy=0):
        return ((x + dx) % 4) * 4 + ((h + dh) % 2) * 2 + (y + dy) % 2

    plane_step(2)
    q = plane_id()
    for i, (a, b, d) in enumerate(PLANE):
        start(WS.at[plane_id(a, b, d)], R1.at[i], psend.at[i], precv.at[i], dev(dh=a, dx=b, dy=d))

    def term(j):
        return dot(block(j), (G1[...], G2[...]), 0, 0)

    TN[...] = term(NCOLS)
    for p in range(8):
        TS[p] = term(p * 2 + 1 - k)
    for p in range(8):
        TO[p] = term(p * 2 + k)
    start(TN, RN, nsend.at[1], nrecv.at[1], nxt)
    for p in range(8):
        start(TS.at[p], RB.at[p], tsend.at[p], trecv.at[p], SIB)

    for i in range(15):
        remote(WS.at[0], R1.at[i], psend.at[i], precv.at[i], SIB).wait_recv()
    total = WS[q]
    for i in range(15):
        total = total + R1[i]
    z4, zs = z % 4, z // 4
    ZA[z4] = total
    for i in (2, 3, 1):
        m = (z4 + i) % 4
        start(ZA.at[z4], ZA.at[z4], zasend.at[i - 1], zarecv.at[z4], (h * 32 + zs * 4 + m, c))
    step(4)
    for i in range(1, 4):
        m = (z4 + i) % 4
        remote(ZA.at[m], ZA.at[m], zasend.at[0], zarecv.at[m], SIB).wait_recv()
    ZB[zs] = ((ZA[0] + ZA[1]) + (ZA[2] + ZA[3]))
    for i in FAR:
        m = 3 - z4 if i == 4 else z4
        to = (h * 32 + ((zs + i) % 8) * 4 + m, c)
        start(ZB.at[zs], ZB.at[zs], zbsend.at[i - 1], zbrecv.at[zs], to)

    for p in range(8):
        remote(TS.at[p], RB.at[p], tsend.at[p], trecv.at[p], SIB).wait_recv()
        TO[p] = TO[p] + RB[p]
    cp_id = x * 2 + y
    for i, (dx, dy) in enumerate(CHIPS):
        to = ((x + dx) % 4) * 2 + (y + dy) % 2
        start(TO.at[to], RC.at[i], csend.at[i], crecv.at[i], dev(dx=dx, dy=dy))

    for i in range(1, 8):
        m = (zs + i) % 8
        remote(ZB.at[m], ZB.at[m], zbsend.at[0], zbrecv.at[m], SIB).wait_recv()
    total = ZB[0]
    for i in range(1, 8):
        total = total + ZB[i]
    FW[...] = total
    own_copy = pltpu.make_async_copy(FW, wg_o.at[k * 16 + q], osem.at[2])
    own_copy.start()
    mine = wg_o.at[k * 16 + q]
    for i, (a, b, d) in enumerate(PLANE):
        start(FW, mine, fsend.at[i], frecv.at[q], dev(dh=a, dx=b, dy=d))

    remote(TN, RN, nsend.at[1], nrecv.at[1], nxt).wait_recv()
    for i in range(7):
        remote(TO.at[0], RC.at[i], csend.at[i], crecv.at[i], SIB).wait_recv()
    fg = TO[cp_id] + RN[...]
    for i in range(7):
        fg = fg + RC[i]
    FGV[...] = fg * NB[...]
    fg_copy = pltpu.make_async_copy(FGV, fg_o, osem.at[1])
    fg_copy.start()

    for a, b, d in PLANE:
        o = plane_id(a, b, d)
        part = wg_o.at[k * 16 + o]
        remote(part, part, fsend.at[0], frecv.at[o], SIB).wait_recv()
    own_copy.wait()
    part = wg_o.at[pl.ds(k * 16, 16)]
    start(part, part, wsend.at[1], wrecv.at[1], SIB)
    other = wg_o.at[pl.ds((1 - k) * 16, 16)]
    remote(other, other, wsend.at[1], wrecv.at[1], SIB).wait_recv()
    hid_copy.wait()
    fg_copy.wait()
    for cp in pending:
        cp.wait_send()


def deliver(a, b, c, ao, bo, co, sem):
    copies = [pltpu.make_async_copy(i, o, sem.at[n]) for n, (i, o) in enumerate(((a, ao), (b, bo), (c, co)))]
    for cp in copies:
        cp.start()
    for cp in copies:
        cp.wait()


def local(features, degrees, tiles, coords, counts, weight, cotangent):
    anyspace = pl.BlockSpec(memory_space=pl.ANY)
    D = pltpu.SemaphoreType.DMA
    V = lambda *s: pltpu.VMEM(s, f32)
    B = lambda *s: pltpu.VMEM(s, jnp.bfloat16)
    hidden, feature_grad, weight_grad = pl.pallas_call(
        kernel,
        out_shape=(pltpu.VMEM((T, F), f32), pltpu.VMEM((T, F), f32), pltpu.VMEM((32, 8, F), f32)),
        in_specs=[pl.BlockSpec(memory_space=pltpu.HBM)] * 7,
        out_specs=(anyspace, anyspace, anyspace),
        scratch_shapes=[
            pltpu.VMEM((1, T), jnp.int32), pltpu.SMEM((1, SLOTS), jnp.int32), pltpu.SMEM((1,), jnp.int32),
            V(NCOLS, T, F), V(T, F), V(SLOTS, T, T), B(NCOLS + 1, T, T), B(NCOLS + 1, T, T), V(T, F), V(F, F), V(T, F),
            V(T, F), V(T, F), B(F, F), B(F, F), B(T, F), B(T, F), V(T, F),
            V(T, F), V(T, F), V(16, 8, F), V(15, 8, F), V(4, 8, F), V(8, 8, F), V(8, F),
            V(8, T, F), V(8, T, F), V(8, T, F), V(7, T, F), V(T, F), V(T, F), V(T, F),
            D((7,)), D((48,)), D((NCOLS, 2)), D((2,)), D((2,)), D((2,)), D((2,)), D((15,)), D((15,)),
            D((3,)), D((4,)), D((7,)), D((8,)), D((15,)), D((16,)), D((8,)), D((8,)), D((7,)), D((7,)),
            D((3,)), pltpu.SemaphoreType.REGULAR((4,)), pltpu.SemaphoreType.REGULAR((2,)),
        ],
        compiler_params=pltpu.CompilerParams(
            collective_id=1, has_side_effects=True, vmem_limit_bytes=60 << 20
        ),
        cost_estimate=pl.CostEstimate(flops=400_000_000, bytes_accessed=3_000_000, transcendentals=32768),
        name="layer",
    )(degrees.reshape(1, T), coords, counts, features, tiles.reshape(SLOTS, T, T), weight, cotangent)
    shapes = [(T, F), (T, F), (32, 8, F)]
    outs = [pltpu.with_memory_space_constraint(v, pltpu.VMEM) for v in (hidden, feature_grad, weight_grad)]
    hidden, feature_grad, weight_grad = pl.pallas_call(
        deliver,
        out_shape=tuple(jax.ShapeDtypeStruct(s, f32) for s in shapes),
        in_specs=[anyspace] * 3,
        out_specs=(anyspace,) * 3,
        scratch_shapes=[D((3,))],
        name="deliver",
    )(*outs)
    return hidden, feature_grad, weight_grad.reshape(F, F)


def solution(mesh):
    return jax.shard_map(
        local,
        mesh=mesh,
        in_specs=(
            P(("rows", "cols"), None),
            P(("rows", "cols")),
            P(("rows", "cols"), None, None, None),
            P(("rows", "cols"), None),
            P(("rows", "cols")),
            P(),
            P(("rows", "cols"), None),
        ),
        out_specs=(P(("rows", "cols"), None), P(("rows", "cols"), None), P()),
        check_vma=False,
    )
```
